768 devices in a mesh: row: 32 (over x_lo, y, core), col: 24 (over x_hi, z).
Axes of the slice: x: 4 (x_hi: 2, x_lo: 2; x = x_hi * 2 + x_lo), y: 8, z: 12, core: 2. Of those that a mesh axis runs over, the one named last changes fastest.
Arguments:
- p_blocks: bfloat16 [36864, 128, 128], P(('row', 'col')), may hold values from -6 to 6
- p_positions: int32 [36864], P(('row', 'col')), may hold values from 0 to 127, as said below
- h_blocks: bfloat16 [192, 128, 128], P('col'), may hold values from -0.1875 to 0.1875
- h_rows: int32 [192], replicated, may hold values from 0 to 63, as said below
- keep_mask: int32 [1536, 24], P(('row', 'col')), may hold values 0 or 1
- owner_ids: int32 [1536, 24, 1], P(('row', 'col')), may hold values from 0 to 31; in each aligned block of 48 rows (0 to 47, 48 to 95, ..., all dimensions but the last counted through in order) at most 2 rows name the same one
Outputs:
- owned: bfloat16 [24576, 2, 128, 128], P(('row', 'col'))
The draws below stay inside these ranges and needn't reach their ends.
Inputs may be any that keep to these rules, and one draw needn't show every extreme that they name: `p_positions`: within each group of 48 entries no value repeats. `h_rows`: within each group of 8 entries no value repeats. `owner_ids`: among the 48 blocks of one group of 2 block rows no owner appears more than 2 times.
All inputs are finite; a program needn't handle non-finite values. No bound on the sum of `keep_mask` on one device may be relied on, other than what follows from the above.
Results may differ from the reference program's by a relative error of at most 0.012.
Values may be sent and summed in bfloat16 or wider, within the bound.
No kernel may reach another device: no remote copies, remote signals or barrier semaphores. Data moves between devices by JAX's collectives and lax.ppermute only.
A program may use at most 64 MiB of HBM per device.

```python
import math
import jax
import jax.numpy as jnp
import numpy as np
from jax import lax

BLOCK = 128
RB = 2
KB = 64
NH = 8
NP = 48
SEND_CAP = 2
NRG = 32
NCB = 24
NBR = 1536


def draw_p_positions(key, part):
    key = jax.random.fold_in(key, 11)
    keys = jax.random.split(key, NRG * NCB)
    orders = jax.vmap(lambda single: jax.random.permutation(single, RB * KB))(keys)
    return orders[:, :NP].reshape(-1).astype(jnp.int32)


def draw_h_rows(key, part):
    key = jax.random.fold_in(key, 23)
    keys = jax.random.split(key, NCB)
    orders = jax.vmap(lambda single: jax.random.permutation(single, KB))(keys)
    return orders[:, :NH].reshape(-1).astype(jnp.int32)


def with_ends(values, stream_key, smallest, high):
    extent = values.shape
    place = [jax.random.randint(jax.random.fold_in(stream_key, axis), (), 0, extent[axis]) for axis in range(len(extent))]
    values = values.at[tuple(place)].set(smallest)
    longest = extent.index(max(extent))
    place[longest] = (place[longest] + 1) % extent[longest]
    return values.at[tuple(place)].set(high)


def block_scale(rng, extent, pieces, least, largest):
    factor_of, own = 1.0, jax.random.fold_in(rng, 6)
    for axis_at, shards_of in pieces:
        draws = jnp.exp(jax.random.uniform(jax.random.fold_in(own, axis_at), (shards_of,), jnp.float32, least / len(pieces), largest / len(pieces)))
        factor_of = factor_of * jnp.repeat(draws, extent[axis_at] // shards_of).reshape([-1 if axis == axis_at else 1 for axis in range(len(extent))])
    return factor_of


def deal_out(own_key, own, number, rows, amount, top, limit, skew):
    order = jax.random.permutation(own_key, amount)
    crowded, usual = shares(amount, rows * top, limit, skew, True), shares(amount, rows * top, limit, skew, False)
    places = jnp.arange(amount)

    def named(tallies, turn):
        used = int((tallies > 0).sum())
        fixed = max(1, used // 4)
        shifted = fixed + (places - fixed + turn * (used - fixed)) % max(1, amount - fixed)
        return jnp.zeros((amount,), jnp.int32).at[order[jnp.where(places < fixed, places, shifted)]].set(jnp.asarray(tallies, jnp.int32))

    tallies = jnp.where(number % 4 == 0, named(crowded, number // 4), named(usual, number - number // 4 - 1))
    mixed = jax.random.permutation(jax.random.fold_in(own, 3), amount)
    source_of, sink = mixed[0:amount // 2 * 2:2], mixed[1:amount // 2 * 2:2]
    slack = jnp.minimum(tallies[source_of] - 1, limit - tallies[sink]) // 2
    slack = jnp.where((source_of == order[0]) | (sink == order[0]) | (tallies[sink] == 0), 0, jnp.maximum(slack, 0))
    shifted = jax.random.randint(jax.random.fold_in(own, 4), (amount // 2,), 0, 1 << 20) % (slack + 1)
    tallies = tallies.at[source_of].add(-shifted).at[sink].add(shifted)
    members = jnp.searchsorted(jnp.cumsum(tallies), jnp.arange(rows * top), side="right").astype(jnp.int32)
    grid = members.reshape(top, rows).T
    grid = grid[jax.random.permutation(jax.random.fold_in(own, 1), rows)]
    turn = jax.random.randint(jax.random.fold_in(own, 2), (rows, 1), 0, top)
    return jnp.take_along_axis(grid, (jnp.arange(top)[None, :] + turn) % top, axis=1)


def shares(number_of, total, reach, skew, full):
    loads = [(1 << 20) // math.isqrt(rank ** skew) + 1 for rank in range(1, number_of + 1)]
    largest = reach if full else min(reach, max(-(-total // number_of), total * loads[0] // sum(loads)))
    least = 1 if total - largest >= number_of - 1 else 0
    holding, surplus = [largest] + [least] * (number_of - 1), total - largest - least * (number_of - 1)
    while surplus > 0:
        movable = [i for i in range(1, number_of) if holding[i] < largest] or [i for i in range(1, number_of) if holding[i] < reach]
        whole, budget = sum([loads[i] for i in movable]), surplus
        for i in movable:
            extra = min(reach - holding[i], max(1, budget * loads[i] // whole), surplus)
            holding[i] = holding[i] + extra
            surplus = surplus - extra
    return np.array(holding)


def scatter_about(key, extent, scale, bound, shards=(), kind=jnp.bfloat16):
    entries = jax.random.normal(key, extent, jnp.float32) * scale
    if len(shards) > 0:
        entries = block_scale(key, extent, shards, -0.22, 0.18) * entries
    return jnp.clip(entries, min=-bound, max=bound).astype(kind)


def setup_inputs(seed: int = 0) -> dict:
    splits = jax.random.split(jax.random.key(seed), 7)
    p_blocks = scatter_about(splits[0], (NP * NRG * NCB, BLOCK, BLOCK), 1.0, 6.0, ((0, 768),))
    p_positions = draw_p_positions(jax.random.fold_in(splits[6], 71), 0)
    h_blocks = scatter_about(splits[2], (NH * NCB, BLOCK, BLOCK), (NH * BLOCK) ** -0.5, 0.1875, ((0, 24),))
    h_rows = draw_h_rows(jax.random.fold_in(splits[6], 71), 0)
    keep_mask = with_ends((jax.random.randint(splits[4], (NBR, NCB), 0, 3) < 2).astype(jnp.int32), jax.random.fold_in(splits[4], 1), 0, 1)
    owner_ids_keys = jax.random.split(jax.random.fold_in(splits[5], 1), NBR * NCB // (RB * NCB))
    owner_ids_turns = jax.random.permutation(jax.random.fold_in(splits[5], 3), NBR * NCB // (RB * NCB))
    owner_ids = jax.vmap(lambda own, number: deal_out(jax.random.fold_in(splits[5], 2), own, number, RB * NCB, NRG, 1, SEND_CAP, 2))(owner_ids_keys, owner_ids_turns).reshape((NBR, NCB, 1))
    return {"p_blocks": p_blocks, "p_positions": p_positions, "h_blocks": h_blocks, "h_rows": h_rows, "keep_mask": keep_mask, "owner_ids": owner_ids}


def reference(p_blocks, p_positions, h_blocks, h_rows, keep_mask, owner_ids):
    groups = NRG * NCB
    block_size = BLOCK
    p_values = p_blocks.reshape(groups, NP, block_size, block_size)
    p_where = p_positions.reshape(groups, NP)
    h_values = h_blocks.astype(jnp.float32).reshape(NCB, NH, block_size, block_size)

    def device_product(inputs):
        values_in, index_in = inputs
        slot_ids = (index_in % KB) * RB + index_in // KB
        dense_panel = jnp.zeros((KB * RB, block_size, block_size), jnp.float32)
        dense_panel = dense_panel.at[slot_ids].set(values_in.astype(jnp.float32))
        dense_panel = dense_panel.reshape(KB, RB, block_size, block_size)
        columns = dense_panel[h_rows].reshape(NCB, NH, RB, block_size, block_size)
        product = jnp.einsum('jnrab,jnbc->rjac', columns, h_values)
        return product.astype(jnp.bfloat16)

    blocks = lax.map(device_product, (p_values, p_where))
    keep_flags = keep_mask.reshape(groups, RB, NCB) == 1
    blocks = jnp.where(keep_flags[:, :, :, None, None], blocks, jnp.zeros_like(blocks))
    blocks = blocks.reshape(groups * RB * NCB, block_size, block_size)
    target_owner = owner_ids.reshape(groups, RB * NCB).astype(jnp.int32)
    onehot = (target_owner[:, :, None] == jnp.arange(NRG, dtype=jnp.int32)[None, None, :]).astype(jnp.int32)
    rank_of = jnp.sum((jnp.cumsum(onehot, axis=1) - onehot) * onehot, axis=2).astype(jnp.int32)
    group_ids = jnp.arange(groups, dtype=jnp.int32)[:, None]
    target = (target_owner * NCB + group_ids % NCB) * NRG + group_ids // NCB
    owned = jnp.zeros((NRG * NRG * NCB, SEND_CAP, block_size, block_size), jnp.bfloat16)
    owned = owned.at[target.reshape(-1), rank_of.reshape(-1)].set(blocks)
    return owned
```

```python
import functools

import jax
import jax.numpy as jnp
import numpy as np
from jax import lax
from jax.experimental import pallas as pl
from jax.experimental.pallas import tpu as pltpu
from jax.sharding import PartitionSpec as P

NX, NY, NZ = 4, 8, 12
BS = 128
KB = 64
RB = 2
NH = 8
NCB = 24
NRG = 32
NP = 48
CAP = 2
BOTH = ("row", "col")


def device_of(x, y, z, core):
    x, y, z = x % NX, y % NY, z % NZ
    return ((x % 2) * 2 * NY + y * 2 + core) * NCB + (x // 2) * NZ + z


def pull(steps):
    return [
        (device_of(x + steps[k][0], y + steps[k][1], z + steps[k][2], k), device_of(x, y, z, k))
        for x in range(NX)
        for y in range(NY)
        for z in range(NZ)
        for k in range(2)
    ]


PLUS_ONE = pull(((1, 0, 0), (0, 0, 1)))
MINUS_ONE = pull(((0, 0, -1), (-1, 0, 0)))
PLUS_TWO = pull(((0, 1, 0), (0, -1, 0)))
OTHER_CORE = [(r, r ^ 1) for r in range(NRG)]


def colour(x, y, z):
    return lax.rem(x + 2 * y + z, 4)


def pick_kernel(where, h_ref, out_ref):
    row = where[0]
    x_lo, y, core = row // (2 * NY), (row // 2) % NY, row % 2
    for d in range(NCB):
        c = colour(2 * (d // NZ) + x_lo, y, d % NZ)
        out_ref[d] = h_ref[2 * c + core]


def product_kernel(where, pos, rows, keep, owner, p_hbm, *refs):
    panels, (out_ref, p_all, place, slot, count, sem) = refs[:8], refs[8:]
    load = pltpu.make_async_copy(p_hbm, p_all.at[pl.ds(0, NP)], sem)
    load.start()
    p_all[NP] = jnp.zeros((BS, BS), jnp.bfloat16)
    out_ref[...] = jnp.zeros_like(out_ref)

    row, col = where[0], where[1]
    x, y, z, core = 2 * (col // NZ) + row // (2 * NY), (row // 2) % NY, col % NZ, row % 2
    c = colour(x, y, z)
    listed = []
    for k in (core, 1 - core):
        for step in (0, 1, 3, 2):
            listed.append(2 * lax.rem(c + step, 4) + k)

    def clear(i, carry):
        place[i] = NP
        return carry

    lax.fori_loop(0, RB * KB, clear, 0)

    def note(i, carry):
        place[pos[i]] = i
        return carry

    lax.fori_loop(0, NP, note, 0)

    def reset(i, carry):
        count[i] = 0
        return carry

    lax.fori_loop(0, NRG, reset, 0)

    def rank(i, carry):
        to = owner[i // NCB, i % NCB]
        used = count[to]
        count[to] = used + 1
        slot[i] = to * CAP + used
        return carry

    lax.fori_loop(0, RB * NCB, rank, 0)
    load.wait()

    def column(j, carry):
        inner = [rows[j * NH + n] for n in listed]
        right = jnp.concatenate([panel[j] for panel in panels], axis=0)
        for i in range(RB):
            left = jnp.concatenate([p_all[place[i * KB + r]] for r in inner], axis=1)
            block = jnp.dot(left, right, preferred_element_type=jnp.float32).astype(jnp.bfloat16)
            out_ref[slot[i * NCB + j]] = jnp.where(keep[i, j] == 1, block, jnp.zeros_like(block))
        return carry

    lax.fori_loop(0, NCB, column, 0)


def local(p_blocks, p_positions, h_blocks, h_rows, keep_mask, owner_ids):
    where = jnp.stack([lax.axis_index("row"), lax.axis_index("col")])
    smem = pl.BlockSpec(memory_space=pltpu.SMEM)
    vmem = pl.BlockSpec(memory_space=pltpu.VMEM)
    panel = jax.ShapeDtypeStruct((NCB, BS, BS), jnp.bfloat16)
    picked = pl.pallas_call(
        pick_kernel, out_shape=panel, in_specs=[smem, vmem], out_specs=vmem, name="pick"
    )(where, h_blocks)
    own = lax.all_to_all(picked, "col", split_axis=0, concat_axis=0, tiled=True)
    mine = [own] + [lax.ppermute(own, BOTH, pairs) for pairs in (PLUS_ONE, MINUS_ONE, PLUS_TWO)]
    theirs = [lax.ppermute(block, "row", OTHER_CORE) for block in mine]
    outgoing = pl.pallas_call(
        product_kernel,
        out_shape=jax.ShapeDtypeStruct((NRG * CAP, BS, BS), jnp.bfloat16),
        in_specs=[smem] * 5 + [pl.BlockSpec(memory_space=pl.ANY)] + [vmem] * 8,
        out_specs=vmem,
        scratch_shapes=[
            pltpu.VMEM((NP + 1, BS, BS), jnp.bfloat16),
            pltpu.SMEM((RB * KB,), jnp.int32),
            pltpu.SMEM((RB * NCB,), jnp.int32),
            pltpu.SMEM((NRG,), jnp.int32),
            pltpu.SemaphoreType.DMA,
        ],
        compiler_params=pltpu.CompilerParams(vmem_limit_bytes=24 * 1024 * 1024),
        name="product",
    )(where, p_positions, h_rows, keep_mask, owner_ids.reshape(RB, NCB), p_blocks, *mine, *theirs)
    outgoing = outgoing.reshape(NRG, CAP, BS, BS)
    return lax.all_to_all(outgoing, "row", split_axis=0, concat_axis=0, tiled=True)


def solution(mesh):
    return jax.shard_map(
        local,
        mesh=mesh,
        in_specs=(
            P(("row", "col"), None, None),
            P(("row", "col")),
            P("col", None, None),
            P(),
            P(("row", "col"), None),
            P(("row", "col"), None, None),
        ),
        out_specs=P(("row", "col"), None, None, None),
        check_vma=False,
    )
```

```python
import functools

import jax
import jax.numpy as jnp
import numpy as np
from jax import lax
from jax.experimental import pallas as pl
from jax.experimental.pallas import tpu as pltpu
from jax.sharding import PartitionSpec as P

NX, NY, NZ = 4, 8, 12
BS = 128
KB = 64
RB = 2
NH = 8
NCB = 24
NRG = 32
NP = 48
CAP = 2
BOTH = ("row", "col")


def device_of(x, y, z, core):
    x, y, z = x % NX, y % NY, z % NZ
    return ((x % 2) * 2 * NY + y * 2 + core) * NCB + (x // 2) * NZ + z


def pull(steps):
    return [
        (device_of(x + steps[k][0], y + steps[k][1], z + steps[k][2], k), device_of(x, y, z, k))
        for x in range(NX)
        for y in range(NY)
        for z in range(NZ)
        for k in range(2)
    ]


PLUS_ONE = pull(((1, 0, 0), (0, 0, 1)))
MINUS_ONE = pull(((0, 0, -1), (-1, 0, 0)))
PLUS_TWO = pull(((0, 1, 0), (0, -1, 0)))
OTHER_CORE = [(r, r ^ 1) for r in range(NRG)]
UP_Z = pull(((-1, 0, 1), (-1, 0, 1)))
DOWN_Z = pull(((1, 0, -1), (1, 0, -1)))
STRIDE = 3
PER = NCB // STRIDE
THIRDS = [[h * NZ + m + STRIDE * i for h in range(2) for i in range(NZ // STRIDE)] for m in range(STRIDE)]


def colour(x, y, z):
    return lax.rem(x + 2 * y + z, 4)


def place_of(where):
    row, col = where[0], where[1]
    return 2 * (col // NZ) + row // (2 * NY), lax.rem(row // 2, NY), lax.rem(col, NZ), lax.rem(row, 2)


def pick_kernel(where, h_ref, out_ref):
    x, y, z, core = place_of(where)
    x, z = lax.rem(x, 2), lax.rem(z, STRIDE)
    for d in range(PER):
        c = colour(2 * (d // (PER // 2)) + x, y, z + STRIDE * (d % (PER // 2)))
        out_ref[d] = h_ref[2 * c + core]


def product_kernel(where, pos, rows, keep, owner, p_hbm, *refs):
    panels, (out_ref, p_all, place, slot, count, sem) = refs[:8], refs[8:]
    load = pltpu.make_async_copy(p_hbm, p_all.at[pl.ds(0, NP)], sem)
    load.start()
    p_all[NP] = jnp.zeros((BS, BS), jnp.bfloat16)
    out_ref[...] = jnp.zeros_like(out_ref)

    x, y, z, core = place_of(where)
    c = colour(x, y, z)
    listed, first = [], []
    for k in (core, 1 - core):
        for step, dz in ((0, 0), (1, k), (3, 2 * (1 - k)), (2, 0)):
            listed.append(2 * lax.rem(c + step, 4) + k)
            first.append(lax.rem(z + dz, STRIDE))

    for i in range(RB * KB):
        place[i] = NP
    for i in range(NP):
        place[pos[i]] = i
    for i in range(NRG):
        count[i] = 0
    for i in range(RB * NCB):
        to = owner[i // NCB, i % NCB]
        used = count[to]
        count[to] = used + 1
        slot[i] = to * CAP + used
    load.wait()

    def column(j, carry):
        jz = lax.rem(j, NZ)
        base = (j // NZ) * (PER // 2) + jz // STRIDE
        at = [lax.rem(jz + STRIDE - f, STRIDE) * PER + base for f in first]
        inner = [rows[j * NH + n] for n in listed]
        right = jnp.concatenate([panel[u] for panel, u in zip(panels, at)], axis=0)
        left = jnp.concatenate(
            [
                jnp.concatenate([p_all[place[i * KB + r]] for r in inner], axis=1)
                for i in range(RB)
            ],
            axis=0,
        )
        both = jnp.dot(left, right, preferred_element_type=jnp.float32).astype(jnp.bfloat16)
        for i in range(RB):
            block = both[i * BS : (i + 1) * BS]
            out_ref[slot[i * NCB + j]] = jnp.where(keep[i, j] == 1, block, jnp.zeros_like(block))
        return carry

    lax.fori_loop(0, NCB, column, 0, unroll=4)


def local(p_blocks, p_positions, h_blocks, h_rows, keep_mask, owner_ids):
    where = jnp.stack([lax.axis_index("row"), lax.axis_index("col")])
    smem = pl.BlockSpec(memory_space=pltpu.SMEM)
    vmem = pl.BlockSpec(memory_space=pltpu.VMEM)
    panel = jax.ShapeDtypeStruct((PER, BS, BS), jnp.bfloat16)
    picked = pl.pallas_call(
        pick_kernel, out_shape=panel, in_specs=[smem, vmem], out_specs=vmem, name="pick"
    )(where, h_blocks)
    third = lax.all_to_all(
        picked, "col", split_axis=0, concat_axis=0, axis_index_groups=THIRDS, tiled=True
    )
    own = jnp.concatenate([third] + [lax.ppermute(third, BOTH, pairs) for pairs in (UP_Z, DOWN_Z)])
    mine = [own] + [lax.ppermute(own, BOTH, pairs) for pairs in (PLUS_ONE, MINUS_ONE, PLUS_TWO)]
    theirs = [lax.ppermute(block, "row", OTHER_CORE) for block in mine]
    outgoing = pl.pallas_call(
        product_kernel,
        out_shape=jax.ShapeDtypeStruct((NRG * CAP, BS, BS), jnp.bfloat16),
        in_specs=[smem] * 5 + [pl.BlockSpec(memory_space=pl.ANY)] + [vmem] * 8,
        out_specs=vmem,
        scratch_shapes=[
            pltpu.VMEM((NP + 1, BS, BS), jnp.bfloat16),
            pltpu.SMEM((RB * KB,), jnp.int32),
            pltpu.SMEM((RB * NCB,), jnp.int32),
            pltpu.SMEM((NRG,), jnp.int32),
            pltpu.SemaphoreType.DMA,
        ],
        compiler_params=pltpu.CompilerParams(vmem_limit_bytes=24 * 1024 * 1024),
        name="product",
    )(where, p_positions, h_rows, keep_mask, owner_ids.reshape(RB, NCB), p_blocks, *mine, *theirs)
    outgoing = outgoing.reshape(NRG, CAP, BS, BS)
    return lax.all_to_all(outgoing, "row", split_axis=0, concat_axis=0, tiled=True)


def solution(mesh):
    return jax.shard_map(
        local,
        mesh=mesh,
        in_specs=(
            P(("row", "col"), None, None),
            P(("row", "col")),
            P("col", None, None),
            P(),
            P(("row", "col"), None),
            P(("row", "col"), None, None),
        ),
        out_specs=P(("row", "col"), None, None, None),
        check_vma=False,
    )
```

```python
import functools

import jax
import jax.numpy as jnp
import numpy as np
from jax import lax
from jax.experimental import pallas as pl
from jax.experimental.pallas import tpu as pltpu
from jax.sharding import PartitionSpec as P

NX, NY, NZ = 4, 8, 12
BS = 128
KB = 64
RB = 2
NH = 8
NCB = 24
NRG = 32
NP = 48
CAP = 2
BOTH = ("row", "col")


def device_of(x, y, z, core):
    x, y, z = x % NX, y % NY, z % NZ
    return ((x % 2) * 2 * NY + y * 2 + core) * NCB + (x // 2) * NZ + z


def pull(steps):
    return [
        (device_of(x + steps[k][0], y + steps[k][1], z + steps[k][2], k), device_of(x, y, z, k))
        for x in range(NX)
        for y in range(NY)
        for z in range(NZ)
        for k in range(2)
    ]


PLUS_ONE = pull(((1, 0, 0), (0, 0, 1)))
MINUS_ONE = pull(((0, 0, -1), (-1, 0, 0)))
PLUS_TWO = pull(((0, 1, 0), (0, -1, 0)))
OTHER_CORE = [(r, r ^ 1) for r in range(NRG)]
NEXT_Z = pull(((-1, 0, 1), (1, 0, -1)))
STRIDE = 2
PER = NCB // STRIDE
HALVES = [
    [h * NZ + m + STRIDE * i for p in range(2) for h in range(2) for i in range(p ^ h, NZ // STRIDE, 2)]
    for m in range(STRIDE)
]


def colour(x, y, z):
    return lax.rem(x + 2 * y + z, 4)


def place_of(where):
    row, col = where[0], where[1]
    return 2 * (col // NZ) + row // (2 * NY), lax.rem(row // 2, NY), lax.rem(col, NZ), lax.rem(row, 2)


def pick(row, col, h_blocks):
    c = (row >> 4) + (row & 14) + (col & 1)
    first, second = (
        lax.dynamic_index_in_dim(h_blocks, 2 * (k & 3) + (row & 1), axis=0) for k in (c, c + 2)
    )
    return jnp.where(jnp.arange(PER)[:, None, None] < PER // 2, first, second)


def product_kernel(where, pos, rows, keep, owner, p_hbm, *refs):
    panels, (out_ref, p_all, place, slot, count, sem) = refs[:8], refs[8:]
    load = pltpu.make_async_copy(p_hbm, p_all.at[pl.ds(0, NP)], sem)
    load.start()
    p_all[NP] = jnp.zeros((BS, BS), jnp.bfloat16)
    out_ref[...] = jnp.zeros_like(out_ref)

    x, y, z, core = place_of(where)
    c = colour(x, y, z)
    listed, first = [], []
    for k in (core, 1 - core):
        for step, dz in ((0, 0), (1, k), (3, 1 - k), (2, 0)):
            listed.append(2 * lax.rem(c + step, 4) + k)
            first.append(lax.rem(z + dz, STRIDE))

    for i in range(RB * KB):
        place[i] = NP
    for i in range(NP):
        place[pos[i]] = i
    for i in range(NRG):
        count[i] = 0
    for i in range(RB * NCB):
        to = owner[i // NCB, i % NCB]
        used = count[to]
        count[to] = used + 1
        slot[i] = to * CAP + used
    load.wait()

    def column(j, carry):
        jz = lax.rem(j, NZ)
        h, i = j // NZ, jz // STRIDE
        base = lax.rem(h + i, 2) * (PER // 2) + h * (PER // 4) + i // 2
        at = [lax.rem(jz + STRIDE - f, STRIDE) * PER + base for f in first]
        inner = [rows[j * NH + n] for n in listed]
        right = jnp.concatenate([panel[u] for panel, u in zip(panels, at)], axis=0)
        left = jnp.concatenate(
            [
                jnp.concatenate([p_all[place[i * KB + r]] for r in inner], axis=1)
                for i in range(RB)
            ],
            axis=0,
        )
        both = jnp.dot(left, right, preferred_element_type=jnp.float32).astype(jnp.bfloat16)
        for i in range(RB):
            block = both[i * BS : (i + 1) * BS]
            out_ref[slot[i * NCB + j]] = jnp.where(keep[i, j] == 1, block, jnp.zeros_like(block))
        return carry

    lax.fori_loop(0, NCB, column, 0, unroll=12)


def local(p_blocks, p_positions, h_blocks, h_rows, keep_mask, owner_ids):
    row, col = lax.axis_index("row"), lax.axis_index("col")
    smem = pl.BlockSpec(memory_space=pltpu.SMEM)
    vmem = pl.BlockSpec(memory_space=pltpu.VMEM)
    half = lax.all_to_all(
        pick(row, col, h_blocks),
        "col",
        split_axis=0,
        concat_axis=0,
        axis_index_groups=HALVES,
        tiled=True,
    )
    own = jnp.concatenate([half, lax.ppermute(half, BOTH, NEXT_Z)])
    mine = [own] + [lax.ppermute(own, BOTH, pairs) for pairs in (PLUS_ONE, MINUS_ONE, PLUS_TWO)]
    theirs = [lax.ppermute(block, "row", OTHER_CORE) for block in mine]
    outgoing = pl.pallas_call(
        product_kernel,
        out_shape=jax.ShapeDtypeStruct((NRG * CAP, BS, BS), jnp.bfloat16),
        in_specs=[smem] * 5 + [pl.BlockSpec(memory_space=pl.ANY)] + [vmem] * 8,
        out_specs=vmem,
        scratch_shapes=[
            pltpu.VMEM((NP + 1, BS, BS), jnp.bfloat16),
            pltpu.SMEM((RB * KB,), jnp.int32),
            pltpu.SMEM((RB * NCB,), jnp.int32),
            pltpu.SMEM((NRG,), jnp.int32),
            pltpu.SemaphoreType.DMA,
        ],
        compiler_params=pltpu.CompilerParams(vmem_limit_bytes=24 * 1024 * 1024),
        name="product",
    )(jnp.stack([row, col]), p_positions, h_rows, keep_mask, owner_ids.reshape(RB, NCB), p_blocks, *mine, *theirs)
    outgoing = outgoing.reshape(NRG, CAP, BS, BS)
    return lax.all_to_all(outgoing, "row", split_axis=0, concat_axis=0, tiled=True)


def solution(mesh):
    return jax.shard_map(
        local,
        mesh=mesh,
        in_specs=(
            P(("row", "col"), None, None),
            P(("row", "col")),
            P("col", None, None),
            P(),
            P(("row", "col"), None),
            P(("row", "col"), None, None),
        ),
        out_specs=P(("row", "col"), None, None, None),
        check_vma=False,
    )
```

```python
import jax
import jax.numpy as jnp
from jax import lax
from jax.experimental import pallas as pl
from jax.experimental.pallas import tpu as pltpu
from jax.sharding import PartitionSpec as P

NX, NY, NZ = 4, 8, 12
BS = 128
KB = 64
RB = 2
NH = 8
NCB = 24
NRG = 32
NP = 48
CAP = 2
PER = NCB // 2
BOTH = ("row", "col")


def device_of(x, y, z, core):
    x, y, z = x % NX, y % NY, z % NZ
    return ((x % 2) * 2 * NY + y * 2 + core) * NCB + (x // 2) * NZ + z


def pull(steps):
    return [
        (device_of(x + steps[k][0], y + steps[k][1], z + steps[k][2], k), device_of(x, y, z, k))
        for x in range(NX)
        for y in range(NY)
        for z in range(NZ)
        for k in range(2)
    ]


NEXT_Z = pull(((-1, 0, 1), (1, 0, -1)))
ALONG_X = pull(((1, 0, 0), (-1, 0, 0)))
ALONG_Z = pull(((0, 0, -1), (0, 0, 1)))
ALONG_Y = pull(((0, 1, 0), (0, -1, 0)))
OTHER_CORE = [(r, r ^ 1) for r in range(NRG)]
HALVES = [
    [h * NZ + m + 2 * i for p in range(2) for h in range(2) for i in range(p ^ h, NZ // 2, 2)]
    for m in range(2)
]


def pick(row, col, h_blocks):
    c = (row >> 4) + (row & 14) + (col & 1)
    first, second = (
        lax.dynamic_index_in_dim(h_blocks, 2 * (k & 3) + (row & 1), axis=0) for k in (c, c + 2)
    )
    return jnp.where(jnp.arange(PER)[:, None, None] < PER // 2, first, second)


def prepare_kernel(pos, owner, p_ref, _, p_all, out_ref, table, count):
    p_all[:NP] = p_ref[...]
    p_all[NP] = jnp.zeros((BS, BS), jnp.bfloat16)
    out_ref[...] = jnp.zeros_like(out_ref)
    for i in range(RB * KB):
        table[i] = NP
    for i in range(NP):
        table[pos[i]] = i
    for i in range(NRG):
        count[i] = 0
    for i in range(RB * NCB):
        to = owner[i // NCB, i % NCB]
        used = count[to]
        count[to] = used + 1
        table[RB * KB + i] = to * CAP + used


def listed_blocks(where):
    row, col = where[0], where[1]
    core = lax.rem(row, 2)
    high = col // NZ
    z = col - NZ * high
    c = 2 * high + row // (2 * NY) + 2 * lax.rem(row // 2, NY) + z
    listed = [
        2 * lax.rem(c + step, 4) + k
        for k in (core, 1 - core)
        for step in (0, 1 + 2 * k, 3 - 2 * k, 2)
    ]
    return listed, lax.rem(z, 2)


def units(parity):
    for q in range(2):
        for h in range(2):
            for i in range(NZ // 2):
                at = ((h + i) % 2) * (PER // 2) + h * (PER // 4) + i // 2
                yield h * NZ + 2 * i + lax.rem(parity + q, 2), q, at


def p_columns(p_all, table, inner):
    return jnp.concatenate(
        [
            jnp.concatenate([p_all[table[r * KB + b]] for b in inner], axis=1)
            for r in range(RB)
        ],
        axis=0,
    )


def most_kernel(where, rows, table, p_all, own, ax, bz, cy, t1, t2, t3, total):
    listed, parity = listed_blocks(where)
    for u, (j, q, at) in enumerate(units(parity)):
        same, other = q * PER + at, (1 - q) * PER + at
        panels = [own[same], ax[same], bz[other], cy[same]]
        panels += [t2[at] if q else t1[at], t2[PER + same], t3[other]]
        left = p_columns(p_all, table, [rows[j * NH + n] for n in listed[:-1]])
        total[u] = jnp.dot(left, jnp.concatenate(panels, axis=0), preferred_element_type=jnp.float32)


def rest_kernel(where, rows, keep, table, p_all, total, t4, _, out_ref):
    listed, parity = listed_blocks(where)
    for u, (j, q, at) in enumerate(units(parity)):
        left = p_columns(p_all, table, [rows[j * NH + listed[-1]]])
        both = total[u] + jnp.dot(left, t4[q * PER + at], preferred_element_type=jnp.float32)
        both = both.astype(jnp.bfloat16)
        for r in range(RB):
            block = both[r * BS : (r + 1) * BS]
            out_ref[table[RB * KB + r * NCB + j]] = jnp.where(
                keep[r, j] == 1, block, jnp.zeros_like(block)
            )


def local(p_blocks, p_positions, h_blocks, h_rows, keep_mask, owner_ids):
    row, col = lax.axis_index("row"), lax.axis_index("col")
    smem = pl.BlockSpec(memory_space=pltpu.SMEM)
    vmem = pl.BlockSpec(memory_space=pltpu.VMEM)
    half = lax.all_to_all(
        pick(row, col, h_blocks),
        "col",
        split_axis=0,
        concat_axis=0,
        axis_index_groups=HALVES,
        tiled=True,
    )
    where = jnp.stack([row, col])
    rest = lax.ppermute(half, BOTH, NEXT_Z)
    t1 = lax.ppermute(half, "row", OTHER_CORE)
    limit = pltpu.CompilerParams(vmem_limit_bytes=24 * 1024 * 1024)
    p_all, empty, table = pl.pallas_call(
        prepare_kernel,
        out_shape=[
            jax.ShapeDtypeStruct((NP + 1, BS, BS), jnp.bfloat16),
            jax.ShapeDtypeStruct((NRG * CAP, BS, BS), jnp.bfloat16),
            jax.ShapeDtypeStruct((RB * KB + RB * NCB,), jnp.int32),
        ],
        in_specs=[smem, smem, vmem, pl.BlockSpec(memory_space=pl.ANY)],
        out_specs=[vmem, vmem, smem],
        scratch_shapes=[pltpu.SMEM((NRG,), jnp.int32)],
        compiler_params=limit,
        name="prepare",
    )(p_positions, owner_ids.reshape(RB, NCB), p_blocks, half)
    own, t1, p_all, empty, table = lax.optimization_barrier(
        (jnp.concatenate([half, rest]), t1, p_all, empty, table)
    )
    ax, bz, cy = (lax.ppermute(own, BOTH, pairs) for pairs in (ALONG_X, ALONG_Z, ALONG_Y))
    t2, t3, t4 = (
        lax.ppermute(x, "row", OTHER_CORE) for x in (jnp.concatenate([rest, ax]), bz, cy)
    )
    total = pl.pallas_call(
        most_kernel,
        out_shape=jax.ShapeDtypeStruct((NCB, RB * BS, BS), jnp.float32),
        in_specs=[smem] * 3 + [vmem] * 8,
        out_specs=vmem,
        compiler_params=limit,
        cost_estimate=pl.CostEstimate(flops=1_400_000_000, bytes_accessed=10_000_000, transcendentals=0),
        name="most",
    )(where, h_rows, table, p_all, own, ax, bz, cy, t1, t2, t3)
    outgoing = pl.pallas_call(
        rest_kernel,
        out_shape=jax.ShapeDtypeStruct((NRG * CAP, BS, BS), jnp.bfloat16),
        in_specs=[smem] * 4 + [vmem] * 4,
        out_specs=vmem,
        input_output_aliases={7: 0},
        compiler_params=limit,
        cost_estimate=pl.CostEstimate(flops=200_000_000, bytes_accessed=5_000_000, transcendentals=0),
        name="rest",
    )(where, h_rows, keep_mask, table, p_all, total, t4, empty)
    outgoing = outgoing.reshape(NRG, CAP, BS, BS)
    return lax.all_to_all(outgoing, "row", split_axis=0, concat_axis=0, tiled=True)


def solution(mesh):
    return jax.shard_map(
        local,
        mesh=mesh,
        in_specs=(
            P(("row", "col"), None, None),
            P(("row", "col")),
            P("col", None, None),
            P(),
            P(("row", "col"), None),
            P(("row", "col"), None, None),
        ),
        out_specs=P(("row", "col"), None, None, None),
        check_vma=False,
    )
```

```python
import jax
import jax.numpy as jnp
from jax import lax
from jax.experimental import pallas as pl
from jax.experimental.pallas import tpu as pltpu
from jax.sharding import PartitionSpec as P

NX, NY, NZ = 4, 8, 12
BS = 128
KB = 64
RB = 2
NH = 8
NCB = 24
NRG = 32
NP = 48
CAP = 2
PARTS = 3
PER = NCB // PARTS
BOTH = ("row", "col")


def device_of(x, y, z, core):
    x, y, z = x % NX, y % NY, z % NZ
    return ((x % 2) * 2 * NY + y * 2 + core) * NCB + (x // 2) * NZ + z


def pull(steps):
    return [
        (device_of(x + steps[k][0], y + steps[k][1], z + steps[k][2], k), device_of(x, y, z, k))
        for x in range(NX)
        for y in range(NY)
        for z in range(NZ)
        for k in range(2)
    ]


UP_Z = pull(((-1, 0, 1), (-1, 0, 1)))
DOWN_Z = pull(((1, 0, -1), (1, 0, -1)))
ALONG_X = pull(((1, 0, 0), (-1, 0, 0)))
ALONG_Z = pull(((0, 0, -1), (0, 0, 1)))
ALONG_Y = pull(((0, 1, 0), (0, -1, 0)))
OTHER_CORE = [(r, r ^ 1) for r in range(NRG)]
THIRDS = [
    [
        h * NZ + m + PARTS * i
        for step in range(4)
        for h in range(2)
        for i in range(NZ // PARTS)
        if (2 * h + 3 * i) % 4 == step
    ]
    for m in range(PARTS)
]


def pick(row, col, h_blocks):
    c = (row >> 4) + (row & 14) + lax.rem(jnp.where(col < NZ, col, col - NZ), PARTS)
    blocks = [
        lax.dynamic_index_in_dim(h_blocks, 2 * ((c + step) & 3) + (row & 1), axis=0)
        for step in range(4)
    ]
    member = jnp.arange(PER)[:, None, None]
    low = jnp.where(member < 2, blocks[0], blocks[1])
    high = jnp.where(member < 6, blocks[2], blocks[3])
    return jnp.where(member < 4, low, high)


def prepare_kernel(pos, owner, _, out_ref, table, count):
    out_ref[...] = jnp.zeros_like(out_ref)
    for i in range(RB * KB):
        table[i] = -1
    for i in range(NP):
        table[pos[i]] = i
    for i in range(NRG):
        count[i] = 0
    for i in range(RB * NCB):
        to = owner[i // NCB, i % NCB]
        used = count[to]
        count[to] = used + 1
        table[RB * KB + i] = to * CAP + used


def listed_blocks(where):
    row, col = where[0], where[1]
    core = lax.rem(row, 2)
    high = col // NZ
    z = col - NZ * high
    c = 2 * high + row // (2 * NY) + 2 * lax.rem(row // 2, NY) + z
    listed = [
        2 * lax.rem(c + step, 4) + k
        for k in (core, 1 - core)
        for step in (0, 1 + 2 * k, 3 - 2 * k, 2)
    ]
    return listed, z, core


def units(z):
    for q in range(PARTS):
        for h in range(2):
            for i in range(NZ // PARTS):
                at = 2 * ((2 * h + 3 * i) % 4) + h
                yield h * NZ + PARTS * i + lax.rem(z + q, PARTS), q, at


def p_columns(p_ref, table, inner):
    def block(place):
        listed = p_ref[jnp.maximum(place, 0)]
        return jnp.where(place >= 0, listed, jnp.zeros_like(listed))

    return jnp.concatenate(
        [
            jnp.concatenate([block(table[r * KB + b]) for b in inner], axis=1)
            for r in range(RB)
        ],
        axis=0,
    )


def most_kernel(where, rows, table, p_ref, own, ax, bz, cy, t1, t2, t3, total):
    listed, z, core = listed_blocks(where)
    for u, (j, q, at) in enumerate(units(z)):
        same = q * PER + at
        below, above = (q + 1) % PARTS * PER + at, (q + 2) % PARTS * PER + at
        from_z = [jnp.where(core == 0, below, above), jnp.where(core == 0, above, below)]
        panels = [own[same], ax[same], bz[from_z[0]], cy[same]]
        panels += [t2[same - PER] if q else t1[at], t2[2 * PER + same], t3[from_z[1]]]
        left = p_columns(p_ref, table, [rows[j * NH + n] for n in listed[:-1]])
        total[u] = jnp.dot(left, jnp.concatenate(panels, axis=0), preferred_element_type=jnp.float32)


def rest_kernel(where, rows, keep, table, p_ref, total, t4, _, out_ref):
    listed, z, _core = listed_blocks(where)
    for u, (j, q, at) in enumerate(units(z)):
        left = p_columns(p_ref, table, [rows[j * NH + listed[-1]]])
        both = total[u] + jnp.dot(left, t4[q * PER + at], preferred_element_type=jnp.float32)
        both = both.astype(jnp.bfloat16)
        for r in range(RB):
            block = both[r * BS : (r + 1) * BS]
            out_ref[table[RB * KB + r * NCB + j]] = jnp.where(
                keep[r, j] == 1, block, jnp.zeros_like(block)
            )


def local(p_blocks, p_positions, h_blocks, h_rows, keep_mask, owner_ids):
    row, col = lax.axis_index("row"), lax.axis_index("col")
    smem = pl.BlockSpec(memory_space=pltpu.SMEM)
    vmem = pl.BlockSpec(memory_space=pltpu.VMEM)
    third = lax.all_to_all(
        pick(row, col, h_blocks),
        "col",
        split_axis=0,
        concat_axis=0,
        axis_index_groups=THIRDS,
        tiled=True,
    )
    where = jnp.stack([row, col])
    rest = [lax.ppermute(third, BOTH, pairs) for pairs in (UP_Z, DOWN_Z)]
    t1 = lax.ppermute(third, "row", OTHER_CORE)
    own, t1 = lax.optimization_barrier((jnp.concatenate([third] + rest), t1))
    ax, bz, cy = (lax.ppermute(own, BOTH, pairs) for pairs in (ALONG_X, ALONG_Z, ALONG_Y))
    limit = pltpu.CompilerParams(vmem_limit_bytes=24 * 1024 * 1024)
    empty, table = pl.pallas_call(
        prepare_kernel,
        out_shape=[
            jax.ShapeDtypeStruct((NRG * CAP, BS, BS), jnp.bfloat16),
            jax.ShapeDtypeStruct((RB * KB + RB * NCB,), jnp.int32),
        ],
        in_specs=[smem, smem, pl.BlockSpec(memory_space=pl.ANY)],
        out_specs=[vmem, smem],
        scratch_shapes=[pltpu.SMEM((NRG,), jnp.int32)],
        compiler_params=limit,
        name="prepare",
    )(p_positions, owner_ids.reshape(RB, NCB), own)
    ax, empty, table = lax.optimization_barrier((ax, empty, table))
    t2, t3, t4 = (
        lax.ppermute(x, "row", OTHER_CORE) for x in (jnp.concatenate(rest + [ax]), bz, cy)
    )
    total = pl.pallas_call(
        most_kernel,
        out_shape=jax.ShapeDtypeStruct((NCB, RB * BS, BS), jnp.float32),
        in_specs=[smem] * 3 + [vmem] * 8,
        out_specs=vmem,
        compiler_params=limit,
        cost_estimate=pl.CostEstimate(flops=1_400_000_000, bytes_accessed=10_000_000, transcendentals=0),
        name="most",
    )(where, h_rows, table, p_blocks, own, ax, bz, cy, t1, t2, t3)
    outgoing = pl.pallas_call(
        rest_kernel,
        out_shape=jax.ShapeDtypeStruct((NRG * CAP, BS, BS), jnp.bfloat16),
        in_specs=[smem] * 4 + [vmem] * 4,
        out_specs=vmem,
        input_output_aliases={7: 0},
        compiler_params=limit,
        cost_estimate=pl.CostEstimate(flops=200_000_000, bytes_accessed=5_000_000, transcendentals=0),
        name="rest",
    )(where, h_rows, keep_mask, table, p_blocks, total, t4, empty)
    outgoing = outgoing.reshape(NRG, CAP, BS, BS)
    return lax.all_to_all(outgoing, "row", split_axis=0, concat_axis=0, tiled=True)


def solution(mesh):
    return jax.shard_map(
        local,
        mesh=mesh,
        in_specs=(
            P(("row", "col"), None, None),
            P(("row", "col")),
            P("col", None, None),
            P(),
            P(("row", "col"), None),
            P(("row", "col"), None, None),
        ),
        out_specs=P(("row", "col"), None, None, None),
        check_vma=False,
    )
```

```python
import jax
import jax.numpy as jnp
from jax import lax
from jax.experimental import pallas as pl
from jax.experimental.pallas import tpu as pltpu
from jax.sharding import PartitionSpec as P

NX, NY, NZ = 4, 8, 12
BS = 128
KB = 64
RB = 2
NH = 8
NCB = 24
NRG = 32
NP = 48
CAP = 2
PARTS = 3
PER = NCB // PARTS
BOTH = ("row", "col")


def device_of(x, y, z, core):
    x, y, z = x % NX, y % NY, z % NZ
    return ((x % 2) * 2 * NY + y * 2 + core) * NCB + (x // 2) * NZ + z


def pull(steps):
    return [
        (device_of(x + steps[k][0], y + steps[k][1], z + steps[k][2], k), device_of(x, y, z, k))
        for x in range(NX)
        for y in range(NY)
        for z in range(NZ)
        for k in range(2)
    ]


UP_Z = pull(((-1, 0, 1), (-1, 0, 1)))
DOWN_Z = pull(((1, 0, -1), (1, 0, -1)))
ALONG_X = pull(((1, 0, 0), (-1, 0, 0)))
ALONG_Z = pull(((0, 0, -1), (0, 0, 1)))
ALONG_Y = pull(((0, 1, 0), (0, -1, 0)))
OTHER_CORE = [(r, r ^ 1) for r in range(NRG)]
THIRDS = [
    [
        h * NZ + m + PARTS * i
        for step in range(4)
        for h in range(2)
        for i in range(NZ // PARTS)
        if (2 * h + 3 * i) % 4 == step
    ]
    for m in range(PARTS)
]


def pick(row, col, h_blocks):
    c = (row >> 4) + (row & 14) + lax.rem(jnp.where(col < NZ, col, col - NZ), PARTS)
    blocks = [
        lax.dynamic_index_in_dim(h_blocks, 2 * ((c + step) & 3) + (row & 1), axis=0)
        for step in range(4)
    ]
    member = jnp.arange(PER)[:, None, None]
    low = jnp.where(member < 2, blocks[0], blocks[1])
    high = jnp.where(member < 6, blocks[2], blocks[3])
    return jnp.where(member < 4, low, high)


def prepare_kernel(pos, owner, _, out_ref, table, count):
    out_ref[...] = jnp.zeros_like(out_ref)
    for i in range(RB * KB):
        table[i] = -1
    for i in range(NP):
        table[pos[i]] = i
    for i in range(NRG):
        count[i] = 0
    for i in range(RB * NCB):
        to = owner[i // NCB, i % NCB]
        used = count[to]
        count[to] = used + 1
        table[RB * KB + i] = to * CAP + used


def listed_blocks(where):
    row, col = where[0], where[1]
    core = lax.rem(row, 2)
    high = col // NZ
    z = col - NZ * high
    c = 2 * high + row // (2 * NY) + 2 * lax.rem(row // 2, NY) + z
    listed = [
        2 * lax.rem(c + step, 4) + k
        for k in (core, 1 - core)
        for step in (0, 1 + 2 * k, 3 - 2 * k, 2)
    ]
    return listed, z, core


def units(z):
    for q in range(PARTS):
        for h in range(2):
            for i in range(NZ // PARTS):
                at = 2 * ((2 * h + 3 * i) % 4) + h
                yield h * NZ + PARTS * i + lax.rem(z + q, PARTS), q, at


def p_columns(p_ref, table, inner):
    def block(place):
        listed = p_ref[jnp.maximum(place, 0)]
        return jnp.where(place >= 0, listed, jnp.zeros_like(listed))

    return jnp.concatenate(
        [
            jnp.concatenate([block(table[r * KB + b]) for b in inner], axis=1)
            for r in range(RB)
        ],
        axis=0,
    )


def z_panel(core, q, at):
    return jnp.where(core == 0, (q + 1) % PARTS, (q + 2) % PARTS) * PER + at


def most_kernel(where, rows, table, p_ref, own, ax, bz, cy, t1, t3, total):
    listed, z, core = listed_blocks(where)
    for u, (j, q, at) in enumerate(units(z)):
        same = q * PER + at
        panels = [own[same], ax[same], bz[z_panel(core, q, at)], cy[same]]
        panels += [t3[z_panel(1 - core, q, at)], t3[NCB + same]]
        held = listed[:4] + listed[6:]
        if q == 0:
            panels.append(t1[at])
            held.append(listed[4])
        left = p_columns(p_ref, table, [rows[j * NH + n] for n in held])
        total[u] = jnp.dot(left, jnp.concatenate(panels, axis=0), preferred_element_type=jnp.float32)


def rest_kernel(where, rows, keep, table, p_ref, total, t2, _, out_ref):
    listed, z, _core = listed_blocks(where)
    for u, (j, q, at) in enumerate(units(z)):
        panels, held = [t2[(PARTS - 1 + q) * PER + at]], [listed[5]]
        if q:
            panels.append(t2[(q - 1) * PER + at])
            held.append(listed[4])
        left = p_columns(p_ref, table, [rows[j * NH + n] for n in held])
        both = total[u] + jnp.dot(
            left, jnp.concatenate(panels, axis=0), preferred_element_type=jnp.float32
        )
        both = both.astype(jnp.bfloat16)
        for r in range(RB):
            block = both[r * BS : (r + 1) * BS]
            out_ref[table[RB * KB + r * NCB + j]] = jnp.where(
                keep[r, j] == 1, block, jnp.zeros_like(block)
            )


def local(p_blocks, p_positions, h_blocks, h_rows, keep_mask, owner_ids):
    row, col = lax.axis_index("row"), lax.axis_index("col")
    smem = pl.BlockSpec(memory_space=pltpu.SMEM)
    vmem = pl.BlockSpec(memory_space=pltpu.VMEM)
    third = lax.all_to_all(
        pick(row, col, h_blocks),
        "col",
        split_axis=0,
        concat_axis=0,
        axis_index_groups=THIRDS,
        tiled=True,
    )
    where = jnp.stack([row, col])
    rest = [lax.ppermute(third, BOTH, pairs) for pairs in (UP_Z, DOWN_Z)]
    t1 = lax.ppermute(third, "row", OTHER_CORE)
    own, t1 = lax.optimization_barrier((jnp.concatenate([third] + rest), t1))
    ax, bz, cy = (lax.ppermute(own, BOTH, pairs) for pairs in (ALONG_X, ALONG_Z, ALONG_Y))
    limit = pltpu.CompilerParams(vmem_limit_bytes=24 * 1024 * 1024)
    empty, table = pl.pallas_call(
        prepare_kernel,
        out_shape=[
            jax.ShapeDtypeStruct((NRG * CAP, BS, BS), jnp.bfloat16),
            jax.ShapeDtypeStruct((RB * KB + RB * NCB,), jnp.int32),
        ],
        in_specs=[smem, smem, pl.BlockSpec(memory_space=pl.ANY)],
        out_specs=[vmem, smem],
        scratch_shapes=[pltpu.SMEM((NRG,), jnp.int32)],
        compiler_params=limit,
        name="prepare",
    )(p_positions, owner_ids.reshape(RB, NCB), own)
    bz, empty, table = lax.optimization_barrier((bz, empty, table))
    t2, t3 = (
        lax.ppermute(jnp.concatenate(x), "row", OTHER_CORE) for x in (rest + [ax], [bz, cy])
    )
    total = pl.pallas_call(
        most_kernel,
        out_shape=jax.ShapeDtypeStruct((NCB, RB * BS, BS), jnp.float32),
        in_specs=[smem] * 3 + [vmem] * 7,
        out_specs=vmem,
        compiler_params=limit,
        cost_estimate=pl.CostEstimate(flops=1_200_000_000, bytes_accessed=10_000_000, transcendentals=0),
        name="most",
    )(where, h_rows, table, p_blocks, own, ax, bz, cy, t1, t3)
    outgoing = pl.pallas_call(
        rest_kernel,
        out_shape=jax.ShapeDtypeStruct((NRG * CAP, BS, BS), jnp.bfloat16),
        in_specs=[smem] * 4 + [vmem] * 4,
        out_specs=vmem,
        input_output_aliases={7: 0},
        compiler_params=limit,
        cost_estimate=pl.CostEstimate(flops=400_000_000, bytes_accessed=5_000_000, transcendentals=0),
        name="rest",
    )(where, h_rows, keep_mask, table, p_blocks, total, t2, empty)
    outgoing = outgoing.reshape(NRG, CAP, BS, BS)
    return lax.all_to_all(outgoing, "row", split_axis=0, concat_axis=0, tiled=True)


def solution(mesh):
    return jax.shard_map(
        local,
        mesh=mesh,
        in_specs=(
            P(("row", "col"), None, None),
            P(("row", "col")),
            P("col", None, None),
            P(),
            P(("row", "col"), None),
            P(("row", "col"), None, None),
        ),
        out_specs=P(("row", "col"), None, None, None),
        check_vma=False,
    )
```

```python
import jax
import jax.numpy as jnp
from jax import lax
from jax.experimental import pallas as pl
from jax.experimental.pallas import tpu as pltpu
from jax.sharding import PartitionSpec as P

NX, NY, NZ = 4, 8, 12
BS = 128
KB = 64
RB = 2
NH = 8
NCB = 24
NRG = 32
NP = 48
CAP = 2
PARTS = 3
PER = NCB // PARTS
BOTH = ("row", "col")


def device_of(x, y, z, core):
    x, y, z = x % NX, y % NY, z % NZ
    return ((x % 2) * 2 * NY + y * 2 + core) * NCB + (x // 2) * NZ + z


def pull(steps):
    return [
        (device_of(x + steps[k][0], y + steps[k][1], z + steps[k][2], k), device_of(x, y, z, k))
        for x in range(NX)
        for y in range(NY)
        for z in range(NZ)
        for k in range(2)
    ]


UP_Z = pull(((-1, 0, 1), (-1, 0, 1)))
DOWN_Z = pull(((1, 0, -1), (1, 0, -1)))
ALONG_X = pull(((1, 0, 0), (-1, 0, 0)))
ALONG_Z = pull(((0, 0, -1), (0, 0, 1)))
ALONG_Y = pull(((0, 1, 0), (0, -1, 0)))
OTHER_CORE = [(r, r ^ 1) for r in range(NRG)]
THIRDS = [
    [
        h * NZ + m + PARTS * i
        for step in range(4)
        for h in range(2)
        for i in range(NZ // PARTS)
        if (2 * h + 3 * i) % 4 == step
    ]
    for m in range(PARTS)
]


def pick(row, col, h_blocks):
    c = (row >> 4) + (row & 14) + lax.rem(jnp.where(col < NZ, col, col - NZ), PARTS)
    blocks = [
        lax.dynamic_index_in_dim(h_blocks, 2 * ((c + step) & 3) + (row & 1), axis=0)
        for step in range(4)
    ]
    member = jnp.arange(PER)[:, None, None]
    low = jnp.where(member < 2, blocks[0], blocks[1])
    high = jnp.where(member < 6, blocks[2], blocks[3])
    return jnp.where(member < 4, low, high)


def prepare_kernel(pos, owner, _, out_ref, table, count):
    out_ref[...] = jnp.zeros_like(out_ref)
    for i in range(RB * KB):
        table[i] = -1
    for i in range(NP):
        table[pos[i]] = i
    for i in range(NRG):
        count[i] = 0
    for i in range(RB * NCB):
        to = owner[i // NCB, i % NCB]
        used = count[to]
        count[to] = used + 1
        table[RB * KB + i] = to * CAP + used


def listed_blocks(where):
    row, col = where[0], where[1]
    core = lax.rem(row, 2)
    high = col // NZ
    z = col - NZ * high
    c = 2 * high + row // (2 * NY) + 2 * lax.rem(row // 2, NY) + z
    listed = [
        2 * lax.rem(c + step, 4) + k
        for k in (core, 1 - core)
        for step in (0, 1 + 2 * k, 3 - 2 * k, 2)
    ]
    return listed, z, core


def units(z):
    for q in range(PARTS):
        for h in range(2):
            for i in range(NZ // PARTS):
                at = 2 * ((2 * h + 3 * i) % 4) + h
                yield h * NZ + PARTS * i + lax.rem(z + q, PARTS), q, at


def p_columns(p_ref, table, inner):
    def block(place):
        listed = p_ref[jnp.maximum(place, 0)]
        return jnp.where(place >= 0, listed, jnp.zeros_like(listed))

    return jnp.concatenate(
        [
            jnp.concatenate([block(table[r * KB + b]) for b in inner], axis=1)
            for r in range(RB)
        ],
        axis=0,
    )


def z_panel(core, q, at):
    return jnp.where(core == 0, (q + 1) % PARTS, (q + 2) % PARTS) * PER + at


def first_kernel(where, rows, table, p_ref, own, t1, total):
    listed, z, _core = listed_blocks(where)
    for u, (j, q, at) in enumerate(units(z)):
        panels, held = [own[q * PER + at]], [listed[0]]
        if q == 0:
            panels.append(t1[at])
            held.append(listed[4])
        left = p_columns(p_ref, table, [rows[j * NH + n] for n in held])
        total[u] = jnp.dot(left, jnp.concatenate(panels, axis=0), preferred_element_type=jnp.float32)


def most_kernel(where, rows, table, p_ref, ax, bz, cy, t3, before, total):
    listed, z, core = listed_blocks(where)
    for u, (j, q, at) in enumerate(units(z)):
        same = q * PER + at
        panels = [ax[same], bz[z_panel(core, q, at)], cy[same]]
        panels += [t3[z_panel(1 - core, q, at)], t3[NCB + same]]
        left = p_columns(p_ref, table, [rows[j * NH + n] for n in listed[1:4] + listed[6:]])
        total[u] = before[u] + jnp.dot(
            left, jnp.concatenate(panels, axis=0), preferred_element_type=jnp.float32
        )


def rest_kernel(where, rows, keep, table, p_ref, total, t2, _, out_ref):
    listed, z, _core = listed_blocks(where)
    for u, (j, q, at) in enumerate(units(z)):
        panels, held = [t2[(PARTS - 1 + q) * PER + at]], [listed[5]]
        if q:
            panels.append(t2[(q - 1) * PER + at])
            held.append(listed[4])
        left = p_columns(p_ref, table, [rows[j * NH + n] for n in held])
        both = total[u] + jnp.dot(
            left, jnp.concatenate(panels, axis=0), preferred_element_type=jnp.float32
        )
        both = both.astype(jnp.bfloat16)
        for r in range(RB):
            block = both[r * BS : (r + 1) * BS]
            out_ref[table[RB * KB + r * NCB + j]] = jnp.where(
                keep[r, j] == 1, block, jnp.zeros_like(block)
            )


def local(p_blocks, p_positions, h_blocks, h_rows, keep_mask, owner_ids):
    row, col = lax.axis_index("row"), lax.axis_index("col")
    smem = pl.BlockSpec(memory_space=pltpu.SMEM)
    vmem = pl.BlockSpec(memory_space=pltpu.VMEM)
    third = lax.all_to_all(
        pick(row, col, h_blocks),
        "col",
        split_axis=0,
        concat_axis=0,
        axis_index_groups=THIRDS,
        tiled=True,
    )
    where = jnp.stack([row, col])
    rest = [lax.ppermute(third, BOTH, pairs) for pairs in (UP_Z, DOWN_Z)]
    t1 = lax.ppermute(third, "row", OTHER_CORE)
    own, t1 = lax.optimization_barrier((jnp.concatenate([third] + rest), t1))
    ax, bz, cy = (lax.ppermute(own, BOTH, pairs) for pairs in (ALONG_X, ALONG_Z, ALONG_Y))
    limit = pltpu.CompilerParams(vmem_limit_bytes=24 * 1024 * 1024)
    empty, table = pl.pallas_call(
        prepare_kernel,
        out_shape=[
            jax.ShapeDtypeStruct((NRG * CAP, BS, BS), jnp.bfloat16),
            jax.ShapeDtypeStruct((RB * KB + RB * NCB,), jnp.int32),
        ],
        in_specs=[smem, smem, pl.BlockSpec(memory_space=pl.ANY)],
        out_specs=[vmem, smem],
        scratch_shapes=[pltpu.SMEM((NRG,), jnp.int32)],
        compiler_params=limit,
        name="prepare",
    )(p_positions, owner_ids.reshape(RB, NCB), own)
    where = jnp.stack([row, col])
    sums = jax.ShapeDtypeStruct((NCB, RB * BS, BS), jnp.float32)
    before = pl.pallas_call(
        first_kernel,
        out_shape=sums,
        in_specs=[smem] * 3 + [vmem] * 3,
        out_specs=vmem,
        compiler_params=limit,
        cost_estimate=pl.CostEstimate(flops=300_000_000, bytes_accessed=5_000_000, transcendentals=0),
        name="first",
    )(where, h_rows, table, p_blocks, own, t1)
    bz, empty, table, before = lax.optimization_barrier((bz, empty, table, before))
    t2, t3 = (
        lax.ppermute(jnp.concatenate(x), "row", OTHER_CORE) for x in (rest + [ax], [bz, cy])
    )
    total = pl.pallas_call(
        most_kernel,
        out_shape=sums,
        in_specs=[smem] * 3 + [vmem] * 6,
        out_specs=vmem,
        input_output_aliases={8: 0},
        compiler_params=limit,
        cost_estimate=pl.CostEstimate(flops=1_200_000_000, bytes_accessed=10_000_000, transcendentals=0),
        name="most",
    )(where, h_rows, table, p_blocks, ax, bz, cy, t3, before)
    outgoing = pl.pallas_call(
        rest_kernel,
        out_shape=jax.ShapeDtypeStruct((NRG * CAP, BS, BS), jnp.bfloat16),
        in_specs=[smem] * 4 + [vmem] * 4,
        out_specs=vmem,
        input_output_aliases={7: 0},
        compiler_params=limit,
        cost_estimate=pl.CostEstimate(flops=400_000_000, bytes_accessed=5_000_000, transcendentals=0),
        name="rest",
    )(where, h_rows, keep_mask, table, p_blocks, total, t2, empty)
    outgoing = outgoing.reshape(NRG, CAP, BS, BS)
    return lax.all_to_all(outgoing, "row", split_axis=0, concat_axis=0, tiled=True)


def solution(mesh):
    return jax.shard_map(
        local,
        mesh=mesh,
        in_specs=(
            P(("row", "col"), None, None),
            P(("row", "col")),
            P("col", None, None),
            P(),
            P(("row", "col"), None),
            P(("row", "col"), None, None),
        ),
        out_specs=P(("row", "col"), None, None, None),
        check_vma=False,
    )
```
